32 devices in a mesh: grp: 2 (over y), exp: 8 (over z, core), lat: 2 (over x).
Axes of the slice: x: 2, y: 2, z: 4, core: 2. Of those that a mesh axis runs over, the one named last changes fastest.
Arguments:
- tokens: bfloat16 [128, 2880], P(('grp', 'exp'), 'lat'), parts along dimension 0, may hold values from -6 to 6
- routes: int32 [128, 4], P(('grp', 'exp')), parts along dimension 0, may hold values from 0 to 7, all different within a row; in each aligned block of 8 rows (0 to 7, 8 to 15, ...) at most 5 rows name the same one
- gates: float32 [128, 4], P(('grp', 'exp')), parts along dimension 0, may hold values from 0.1 to 1
- w_gate: bfloat16 [8, 2880, 1440], P('exp', None, 'lat'), may hold values from -0.109375 to 0.109375
- w_up: bfloat16 [8, 2880, 1440], P('exp', None, 'lat'), may hold values from -0.109375 to 0.109375
- w_down: bfloat16 [8, 1440, 2880], P('exp', 'lat'), may hold values from -0.15625 to 0.15625
- w_enc: bfloat16 [2880, 32768], P('lat', 'exp'), may hold values from -0.109375 to 0.109375
- b_enc: float32 [32768], P('exp'), may hold values from -3 to 3
- w_dec: bfloat16 [32768, 2880], P('exp', 'lat'), may hold values from -0.03125 to 0.03125
- b_dec: float32 [2880], P('lat'), may hold values from -3 to 3
Outputs:
- moe_out: bfloat16 [128, 2880], P(('grp', 'exp'), 'lat'), parts along dimension 0
- codes: bfloat16 [128, 32768], P(('grp', 'lat'), 'exp'), parts along dimension 0
- error: float32 [128, 2880], P(('grp', 'exp'), 'lat'), parts along dimension 0
The draws below stay inside these ranges and needn't reach their ends.
There are 2 independent parts, one for each index of `grp`. The reference program is written for one: setup_inputs(seed, part) draws one part's arguments, and reference() takes and returns one part's arrays. A program takes and returns all parts, laid end to end along the dimension named above; an argument that names none is the same for every part. Nothing has to cross between parts.
Inputs may be any that keep to these rules, and one draw needn't show every extreme that they name: `routes`: each row names 4 different experts and every expert is named by some row. Within each aligned block of 8 rows no expert is named by more than 5 rows; in some block some expert is named by exactly 5 rows.
All inputs are finite; a program needn't handle non-finite values.
Results may differ from the reference program's by a relative error of at most 0.013.
Values may be sent and summed in bfloat16 or wider, within the bound.
A program may use at most 128 MiB of HBM per device.

```python
import math
import jax
import jax.numpy as jnp
import numpy as np
from jax import lax

D = 2880
TOP = 4
EFF = 1440
L = 32768
ROW_DEV = 8
EXPERTS = 8
ROWS = 64
CAP = 5
N_EXP = 8


def levels(key, shape, cuts, smallest, top_value):
    def one(position, blocks):
        draws = jax.random.uniform(jax.random.fold_in(jax.random.fold_in(key, 6), position), (blocks,), jnp.float32, smallest / len(cuts), top_value / len(cuts))
        return jnp.repeat(jnp.exp(draws), shape[position] // blocks).reshape((-1,) + (1,) * (len(shape) - position - 1))

    factor_of = one(*cuts[0])
    for cut in cuts[1:]:
        factor_of = factor_of * one(*cut)
    return factor_of


def assign_block(rng, own, number, rows, amount, top, bound, lean):
    sequence = jax.random.permutation(rng, amount)
    crowded, ordinary = shares(amount, rows * top, bound, lean, True), shares(amount, rows * top, bound, lean, False)
    places = jnp.arange(amount)

    def named(sizes, offset_by):
        used = int((sizes > 0).sum())
        fixed = max(1, used // 4)
        moved = fixed + (places - fixed + offset_by * (used - fixed)) % max(1, amount - fixed)
        return jnp.zeros((amount,), jnp.int32).at[sequence[jnp.where(places < fixed, places, moved)]].set(jnp.asarray(sizes, jnp.int32))

    sizes = jnp.where(number % 4 == 0, named(crowded, number // 4), named(ordinary, number - number // 4 - 1))
    mixed = jax.random.permutation(jax.random.fold_in(own, 3), amount)
    giver, receiver = mixed[0:amount // 2 * 2:2], mixed[1:amount // 2 * 2:2]
    room = jnp.minimum(sizes[giver] - 1, bound - sizes[receiver]) // 2
    room = jnp.where((giver == sequence[0]) | (receiver == sequence[0]) | (sizes[receiver] == 0), 0, jnp.maximum(room, 0))
    moved = jax.random.randint(jax.random.fold_in(own, 4), (amount // 2,), 0, 1 << 20) % (room + 1)
    sizes = sizes.at[giver].add(-moved).at[receiver].add(moved)
    labels = jnp.searchsorted(jnp.cumsum(sizes), jnp.arange(rows * top), side="right").astype(jnp.int32)
    listing = labels.reshape(top, rows).T
    listing = listing[jax.random.permutation(jax.random.fold_in(own, 1), rows)]
    offset_by = jax.random.randint(jax.random.fold_in(own, 2), (rows, 1), 0, top)
    return jnp.take_along_axis(listing, (jnp.arange(top)[None, :] + offset_by) % top, axis=1)


def shares(count, total, bound, lean, full):
    loads = [(1 << 20) // math.isqrt(rank ** lean) + 1 for rank in range(1, count + 1)]
    largest = bound if full else min(bound, max(-(-total // count), total * loads[0] // sum(loads)))
    least = 1 if total - largest >= count - 1 else 0
    counts, surplus = [largest] + [least] * (count - 1), total - largest - least * (count - 1)
    while surplus > 0:
        candidates = [i for i in range(1, count) if counts[i] < largest] or [i for i in range(1, count) if counts[i] < bound]
        mass, left = sum([loads[i] for i in candidates]), surplus
        for i in candidates:
            addition = min(bound - counts[i], max(1, left * loads[i] // mass), surplus)
            counts[i] = counts[i] + addition
            surplus = surplus - addition
    return np.array(counts)


def bell_draw(key, shape, deviation, limit, shards=(), held_as=jnp.bfloat16):
    loudness = levels(key, shape, shards, -0.22, 0.18) if shards else 1.0
    array = jax.random.normal(key, shape, jnp.float32) * deviation * loudness
    return jnp.minimum(jnp.maximum(array, -limit), limit).astype(held_as)


def setup_inputs(seed: int = 0, part: int = 0) -> dict:
    splits = jax.random.split(jax.random.key(seed), 11)
    part_keys = jax.random.split(jax.random.fold_in(splits[10], part), 11)
    tokens = bell_draw(part_keys[0], (ROWS, D), 1.0, 6.0, ((0, 8), (1, 2)))
    routes_keys = jax.random.split(jax.random.fold_in(part_keys[1], 1), ROWS // ROW_DEV)
    routes_turns = jax.random.permutation(jax.random.fold_in(part_keys[1], 3), ROWS // ROW_DEV)
    routes = jax.vmap(lambda own, number: assign_block(jax.random.fold_in(part_keys[1], 2), own, number, ROW_DEV, EXPERTS, TOP, CAP, 1))(routes_keys, routes_turns).reshape((ROWS, TOP))
    gates = jnp.clip(0.1 + 0.9 * jax.random.uniform(part_keys[2], (ROWS, TOP), jnp.float32) ** levels(part_keys[2], (ROWS, TOP), ((0, 8),), -0.2, 0.2), 0.1, 1.0)
    w_gate = bell_draw(splits[3], (EXPERTS, D, EFF), D ** -0.5, 0.109375, ((0, 8), (2, 2)))
    w_up = bell_draw(splits[4], (EXPERTS, D, EFF), D ** -0.5, 0.109375, ((0, 8), (2, 2)))
    w_down = bell_draw(splits[5], (EXPERTS, EFF, D), EFF ** -0.5, 0.15625, ((0, 8), (1, 2)))
    w_enc = bell_draw(splits[6], (D, L), D ** -0.5, 0.109375, ((0, 2), (1, 8)))
    b_enc = bell_draw(splits[7], (L,), 0.5, 3.0, ((0, 8),), jnp.float32)
    w_dec = bell_draw(splits[8], (L, D), L ** -0.5, 0.03125, ((0, 8), (1, 2)))
    b_dec = bell_draw(splits[9], (D,), 0.5, 3.0, ((0, 2),), jnp.float32)
    return {"tokens": tokens, "routes": routes, "gates": gates, "w_gate": w_gate, "w_up": w_up, "w_down": w_down, "w_enc": w_enc, "b_enc": b_enc, "w_dec": w_dec, "b_dec": b_dec}


def swiglu_expert(packed):
    buffer, gate_w, up_w, down_w = packed
    gate_sum = jnp.dot(buffer, gate_w, preferred_element_type=jnp.float32)
    up_sum = jnp.dot(buffer, up_w, preferred_element_type=jnp.float32)
    hidden = (gate_sum * jax.nn.sigmoid(1.702 * gate_sum) * (up_sum + 1.0)).astype(jnp.bfloat16)
    return jnp.dot(hidden, down_w, preferred_element_type=jnp.float32)


def reference(tokens, routes, gates, w_gate, w_up, w_down, w_enc, b_enc, w_dec, b_dec):
    flat_expert = routes.reshape(N_EXP, ROW_DEV * TOP).astype(jnp.int32)
    onehot = (flat_expert[:, :, None] == jnp.arange(EXPERTS, dtype=jnp.int32)[None, None, :]).astype(jnp.int32)
    before = jnp.cumsum(onehot, axis=1) - onehot
    rank_in = jnp.sum(before * onehot, axis=2).astype(jnp.int32)
    source = jnp.arange(N_EXP, dtype=jnp.int32)[:, None]
    slot_index = (flat_expert * (N_EXP * CAP) + source * CAP + rank_in).reshape(-1).astype(jnp.int32)
    repeated = jnp.repeat(tokens, TOP, axis=0)
    buffer = jnp.zeros((EXPERTS * N_EXP * CAP, D), jnp.bfloat16).at[slot_index].set(repeated)
    buffer = buffer.reshape(EXPERTS, N_EXP * CAP, D)
    outputs = lax.map(swiglu_expert, (buffer, w_gate, w_up, w_down))
    picked = jnp.take(outputs.reshape(EXPERTS * N_EXP * CAP, D), slot_index, axis=0).reshape(ROWS, TOP, D)
    moe_out = jnp.sum(picked * gates[:, :, None], axis=1).astype(jnp.bfloat16)
    pre = jnp.dot(tokens, w_enc, preferred_element_type=jnp.float32) + b_enc[None, :]
    codes = jnp.maximum(pre, 0.0).astype(jnp.bfloat16)
    recon = jnp.dot(codes, w_dec, preferred_element_type=jnp.float32) + b_dec[None, :]
    error = moe_out.astype(jnp.float32) - recon
    return (moe_out, codes, error)
```

```python
import functools

import jax
import jax.numpy as jnp
from jax import lax
from jax.experimental import pallas as pl
from jax.experimental.pallas import tpu as pltpu
from jax.sharding import PartitionSpec as P

MESH = pl.DeviceIdType.MESH
F32 = jnp.float32
BF16 = jnp.bfloat16
CHUNKS = 4


def dot_nt(a, b):
    return lax.dot_general(a, b, (((1,), (1,)), ((), ())), preferred_element_type=F32)


def kernel(
    E, NL,
    tok, routes, gates, wenc, benc, wg, wu, wd, wdec, bdec,
    moe_ref, codes_ref, err_ref,
    wenc_v, wg_v, wu_v, wd_v, wdec_v,
    xall, xs, psc, own, psend, precv, call,
    phs, msend, mrecv, ms, mbs, mbr, racc, ras, rar, rbs, rbr,
    wsem, gs, gr, fs, fr, ps, pr, cs, cr, hs, hr, bs, br, as_, ar, zs, zr,
):
    R, Dl = tok.shape
    NC = CHUNKS
    Lc = codes_ref.shape[1]
    CW = Lc // NC
    T = E * R
    Tl = T // NL
    N1 = ras.shape[2]
    me = lax.axis_index("exp")
    l = lax.axis_index("lat")

    def peer(d):
        return lax.rem(me + d, E)

    def src(d):
        return lax.rem(me - d + E, E)

    def lpeer(d):
        return lax.rem(l + d, NL)

    def lsrc(d):
        return lax.rem(l - d + NL, NL)

    bar = pltpu.get_barrier_semaphore()
    for d in range(1, E):
        pl.semaphore_signal(bar, inc=1, device_id={"exp": peer(d)}, device_id_type=MESH)
    for d in range(1, NL):
        pl.semaphore_signal(bar, inc=1, device_id={"lat": lpeer(d)}, device_id_type=MESH)

    w_enc = [
        pltpu.make_async_copy(wenc.at[:, pl.ds(c * CW, CW)], wenc_v.at[c], wsem.at[c])
        for c in range(NC)
    ]
    w_g = pltpu.make_async_copy(wg, wg_v, wsem.at[NC])
    w_u = pltpu.make_async_copy(wu, wu_v, wsem.at[NC + 1])
    w_d = pltpu.make_async_copy(wd, wd_v, wsem.at[NC + 2])
    w_dec = [
        pltpu.make_async_copy(wdec.at[:, pl.ds(c * CW, CW)], wdec_v.at[c], wsem.at[NC + 3 + c])
        for c in range(NC)
    ]
    for w in w_enc + [w_g, w_u, w_d] + w_dec:
        w.start()

    xall[l, me] = tok[...]
    pl.semaphore_wait(bar, E - 1 + NL - 1)

    def to_exp(d, source, dest, ssem, rsem):
        return pltpu.make_async_remote_copy(
            src_ref=source, dst_ref=dest, send_sem=ssem, recv_sem=rsem,
            device_id={"exp": peer(d)}, device_id_type=MESH,
        )

    def to_lat(d, source, dest, ssem, rsem):
        return pltpu.make_async_remote_copy(
            src_ref=source, dst_ref=dest, send_sem=ssem, recv_sem=rsem,
            device_id={"lat": lpeer(d)}, device_id_type=MESH,
        )

    def g_copy(d):
        return to_exp(d, tok, xall.at[l, me], gs.at[d], gr.at[d])

    def g_in(d):
        return to_exp(d, tok, xall.at[l, src(d)], gs.at[d], gr.at[d])

    def f_copy(k, d):
        slot = src(k)
        return to_lat(d, xall.at[l, slot], xall.at[l, slot], fs.at[k, d], fr.at[k, d])

    def f_in(k, d):
        slot = src(k)
        return to_lat(d, xall.at[lsrc(d), slot], xall.at[lsrc(d), slot], fs.at[k, d], fr.at[k, d])

    for d in range(1, E):
        g_copy(d).start()
    for d in range(1, NL):
        f_copy(0, d).start()
    for k in range(1, E):
        g_in(k).wait_recv()
        for d in range(1, NL):
            f_copy(k, d).start()

    def rows_of(q):
        for i in range(E):
            xs[i * R:(i + 1) * R, :] = xall[q, i].astype(F32)
        return xs[...]

    def p_copy(c, d):
        return to_lat(d, psend.at[c, d], precv.at[c, d], ps.at[c, d], pr.at[c, d])

    x_own = rows_of(l).astype(BF16)
    for c in range(NC):
        w_enc[c].wait()
        part = jnp.dot(x_own, wenc_v[c], preferred_element_type=F32)
        for q in range(NL):
            psc[q] = part[q * Tl:(q + 1) * Tl, :]
        for d in range(1, NL):
            psend[c, d] = psc[lpeer(d)].astype(BF16)
            p_copy(c, d).start()
        own[c] = psc[l]

    for k in range(E):
        for d in range(1, NL):
            f_in(k, d).wait_recv()
    x_full = jnp.concatenate([rows_of(q) for q in range(NL)], axis=1).astype(BF16)
    w_g.wait()
    gate_sum = dot_nt(x_full, wg_v[...])
    w_u.wait()
    up_sum = dot_nt(x_full, wu_v[...])
    hidden = (gate_sum * jax.nn.sigmoid(1.702 * gate_sum) * (up_sum + 1.0)).astype(BF16)

    def c_copy(c, d):
        return to_lat(d, call.at[c, l], call.at[c, l], cs.at[c, d], cr.at[c, d])

    def c_in(c, d):
        return to_lat(d, call.at[c, lsrc(d)], call.at[c, lsrc(d)], cs.at[c, d], cr.at[c, d])

    for c in range(NC):
        pre = own[c]
        for d in range(1, NL):
            p_copy(c, d).wait_recv()
            pre = pre + precv[c, d].astype(F32)
        code = jnp.maximum(pre + benc[:, c * CW:(c + 1) * CW], 0.0).astype(BF16)
        call[c, l] = code
        codes_ref[:, c * CW:(c + 1) * CW] = code
        for d in range(1, NL):
            c_copy(c, d).start()

    def h_copy(d):
        return to_lat(d, msend.at[d], mrecv.at[d], hs.at[d], hr.at[d])

    w_d.wait()
    part = jnp.dot(hidden, wd_v[...], preferred_element_type=F32)
    for q in range(NL):
        phs[q] = part[:, q * Dl:(q + 1) * Dl]
    for d in range(1, NL):
        msend[d] = phs[lpeer(d)].astype(BF16)
        h_copy(d).start()

    def a_copy(d):
        return to_exp(d, ras.at[peer(d)], rar.at[d], as_.at[d], ar.at[d])

    def z_copy(d):
        return to_exp(d, rbs.at[peer(d)], rbr.at[d], zs.at[d], zr.at[d])

    def b_copy(d):
        return to_exp(d, mbs.at[peer(d)], mbr.at[d], bs.at[d], br.at[d])

    def codes_of(c):
        return call[c].reshape(T, CW)

    for c in range(NC):
        for d in range(1, NL):
            c_in(c, d).wait_recv()
        w_dec[c].wait()
        term = dot_nt(codes_of(c), wdec_v[c, 0:N1, :])
        if c == 0:
            racc[:, 0:N1] = term
        else:
            racc[:, 0:N1] += term
    for i in range(E):
        ras[i] = racc[i * R:(i + 1) * R, 0:N1].astype(BF16)
    for d in range(1, E):
        a_copy(d).start()

    total = phs[l]
    for d in range(1, NL):
        h_copy(d).wait_recv()
        total = total + mrecv[d].astype(F32)
    ms[...] = total
    for i in range(E):
        mbs[i] = ms[i * R:(i + 1) * R, :].astype(BF16)
    for d in range(1, E):
        b_copy(d).start()

    for c in range(NC):
        term = dot_nt(codes_of(c), wdec_v[c, N1:Dl, :])
        if c == 0:
            racc[:, N1:Dl] = term
        else:
            racc[:, N1:Dl] += term
    for i in range(E):
        rbs[i] = racc[i * R:(i + 1) * R, N1:Dl].astype(BF16)
    for d in range(1, E):
        z_copy(d).start()

    eye = lax.broadcasted_iota(jnp.int32, (R, R), 0) == lax.broadcasted_iota(jnp.int32, (R, R), 1)

    def weight_of(e):
        line = jnp.sum(jnp.where(routes[...] == e, gates[...], 0.0), axis=0, keepdims=True)
        return jnp.sum(jnp.where(eye, jnp.broadcast_to(line, (R, R)), 0.0), axis=1, keepdims=True)

    mine = pl.ds(pl.multiple_of(me * R, R), R)
    moe = weight_of(me) * ms[mine, :]
    for d in range(1, E):
        b_copy(d).wait_recv()
        moe = moe + weight_of(src(d)) * mbr[d].astype(F32)
    moe = moe.astype(BF16)
    moe_ref[...] = moe
    err_ref[...] = moe.astype(F32) - bdec[...]

    first = racc[mine, 0:N1]
    for d in range(1, E):
        a_copy(d).wait_recv()
        first = first + rar[d].astype(F32)
    err_ref[:, 0:N1] = err_ref[:, 0:N1] - first
    last = racc[mine, N1:Dl]
    for d in range(1, E):
        z_copy(d).wait_recv()
        last = last + rbr[d].astype(F32)
    err_ref[:, N1:Dl] = err_ref[:, N1:Dl] - last

    for d in range(1, E):
        g_copy(d).wait_send()
        a_copy(d).wait_send()
        b_copy(d).wait_send()
        z_copy(d).wait_send()
    for d in range(1, NL):
        for k in range(E):
            f_copy(k, d).wait_send()
        for c in range(NC):
            p_copy(c, d).wait_send()
            c_copy(c, d).wait_send()
        h_copy(d).wait_send()


def per_device(E, NL, tokens, routes, gates, w_gate, w_up, w_down, w_enc, b_enc, w_dec, b_dec):
    R, Dl = tokens.shape
    D = w_down.shape[2]
    F = w_down.shape[1]
    Lc = w_enc.shape[1]
    NC = CHUNKS
    CW = Lc // NC
    T = E * R
    Tl = T // NL
    N1 = pl.cdiv(pl.cdiv(Dl, 2), 128) * 128
    N2 = Dl - N1
    hbm = pl.BlockSpec(memory_space=pl.ANY)
    vmem = pl.BlockSpec(memory_space=pltpu.VMEM)
    dma = pltpu.SemaphoreType.DMA
    return pl.pallas_call(
        functools.partial(kernel, E, NL),
        out_shape=(
            jax.ShapeDtypeStruct((R, Dl), BF16),
            jax.ShapeDtypeStruct((Tl, Lc), BF16),
            jax.ShapeDtypeStruct((R, Dl), F32),
        ),
        in_specs=[vmem, vmem, vmem, hbm, vmem, hbm, hbm, hbm, hbm, vmem],
        out_specs=(vmem, vmem, vmem),
        scratch_shapes=[
            pltpu.VMEM((NC, Dl, CW), BF16),
            pltpu.VMEM((F, D), BF16),
            pltpu.VMEM((F, D), BF16),
            pltpu.VMEM((F, D), BF16),
            pltpu.VMEM((NC, Dl, CW), BF16),
            pltpu.VMEM((NL, E, R, Dl), BF16),
            pltpu.VMEM((T, Dl), F32),
            pltpu.VMEM((NL, Tl, CW), F32),
            pltpu.VMEM((NC, Tl, CW), F32),
            pltpu.VMEM((NC, NL, Tl, CW), BF16),
            pltpu.VMEM((NC, NL, Tl, CW), BF16),
            pltpu.VMEM((NC, NL, Tl, CW), BF16),
            pltpu.VMEM((NL, T, Dl), F32),
            pltpu.VMEM((NL, T, Dl), BF16),
            pltpu.VMEM((NL, T, Dl), BF16),
            pltpu.VMEM((T, Dl), F32),
            pltpu.VMEM((E, R, Dl), BF16),
            pltpu.VMEM((E, R, Dl), BF16),
            pltpu.VMEM((T, Dl), F32),
            pltpu.VMEM((E, R, N1), BF16),
            pltpu.VMEM((E, R, N1), BF16),
            pltpu.VMEM((E, R, N2), BF16),
            pltpu.VMEM((E, R, N2), BF16),
            dma((2 * NC + 3,)),
            dma((E,)), dma((E,)),
            dma((E, NL)), dma((E, NL)),
            dma((NC, NL)), dma((NC, NL)),
            dma((NC, NL)), dma((NC, NL)),
            dma((NL,)), dma((NL,)),
            dma((E,)), dma((E,)),
            dma((E,)), dma((E,)),
            dma((E,)), dma((E,)),
        ],
        compiler_params=pltpu.CompilerParams(
            collective_id=0, has_side_effects=True, vmem_limit_bytes=58 * 1024 * 1024
        ),
    )(
        tokens, routes.T, gates.T, w_enc, b_enc.reshape(1, -1),
        w_gate[0].T, w_up[0].T, w_down[0], w_dec.T, b_dec.reshape(1, -1),
    )


def solution(mesh):
    placed = (
        P(("grp", "exp"), "lat"),
        P(("grp", "exp"), None),
        P(("grp", "exp"), None),
        P("exp", None, "lat"),
        P("exp", None, "lat"),
        P("exp", "lat", None),
        P("lat", "exp"),
        P("exp"),
        P("exp", "lat"),
        P("lat"),
    )
    return jax.shard_map(
        functools.partial(per_device, mesh.shape["exp"], mesh.shape["lat"]),
        mesh=mesh,
        in_specs=placed,
        out_specs=(P(("grp", "exp"), "lat"), P(("grp", "lat"), "exp"), P(("grp", "exp"), "lat")),
        check_vma=False,
    )
```

```python
import functools

import jax
import jax.numpy as jnp
from jax import lax
from jax.experimental import pallas as pl
from jax.experimental.pallas import tpu as pltpu
from jax.sharding import PartitionSpec as P

MESH = pl.DeviceIdType.MESH
F32 = jnp.float32
BF16 = jnp.bfloat16
CHUNKS = 4


def dot_nt(a, b):
    return lax.dot_general(a, b, (((1,), (1,)), ((), ())), preferred_element_type=F32)


def kernel(
    E, NL,
    tok, routes, gates, wenc, benc, wg, wu, wd, wdec, bdec,
    moe_ref, codes_ref, err_ref,
    wenc_v, wg_v, wu_v, wd_v, wdec_v,
    xall, xs, psc, own, psend, precv, call,
    phs, msend, mrecv, ms, mbs, mbr, racc, ras, rar, rbs, rbr,
    wsem, gs, gr, fs, fr, ps, pr, cs, cr, hs, hr, bs, br, as_, ar, zs, zr,
):
    R, Dl = tok.shape
    NC = CHUNKS
    Lc = codes_ref.shape[1]
    CW = Lc // NC
    T = E * R
    Tl = T // NL
    N1 = ras.shape[2]
    me = lax.axis_index("exp")
    l = lax.axis_index("lat")

    def peer(d):
        return lax.rem(me + d, E)

    def src(d):
        return lax.rem(me - d + E, E)

    def lpeer(d):
        return lax.rem(l + d, NL)

    def lsrc(d):
        return lax.rem(l - d + NL, NL)

    bar = pltpu.get_barrier_semaphore()
    for d in range(1, E):
        pl.semaphore_signal(bar, inc=1, device_id={"exp": peer(d)}, device_id_type=MESH)
    for d in range(1, NL):
        pl.semaphore_signal(bar, inc=1, device_id={"lat": lpeer(d)}, device_id_type=MESH)

    w_enc = [
        pltpu.make_async_copy(wenc.at[:, pl.ds(c * CW, CW)], wenc_v.at[c], wsem.at[c])
        for c in range(NC)
    ]
    w_g = pltpu.make_async_copy(wg, wg_v, wsem.at[NC])
    w_u = pltpu.make_async_copy(wu, wu_v, wsem.at[NC + 1])
    w_d = pltpu.make_async_copy(wd, wd_v, wsem.at[NC + 2])
    w_dec = [
        pltpu.make_async_copy(wdec.at[:, pl.ds(c * CW, CW)], wdec_v.at[c], wsem.at[NC + 3 + c])
        for c in range(NC)
    ]
    for w in w_enc + [w_g, w_u, w_d] + w_dec:
        w.start()

    xall[l, me] = tok[...]
    pl.semaphore_wait(bar, E - 1 + NL - 1)

    def to_exp(d, source, dest, ssem, rsem):
        return pltpu.make_async_remote_copy(
            src_ref=source, dst_ref=dest, send_sem=ssem, recv_sem=rsem,
            device_id={"exp": peer(d)}, device_id_type=MESH,
        )

    def to_lat(d, source, dest, ssem, rsem):
        return pltpu.make_async_remote_copy(
            src_ref=source, dst_ref=dest, send_sem=ssem, recv_sem=rsem,
            device_id={"lat": lpeer(d)}, device_id_type=MESH,
        )

    def g_copy(d):
        return to_exp(d, tok, xall.at[l, me], gs.at[d], gr.at[d])

    def g_in(d):
        return to_exp(d, tok, xall.at[l, src(d)], gs.at[d], gr.at[d])

    def f_copy(k, d):
        slot = src(k)
        return to_lat(d, xall.at[l, slot], xall.at[l, slot], fs.at[k, d], fr.at[k, d])

    def f_in(k, d):
        slot = src(k)
        return to_lat(d, xall.at[lsrc(d), slot], xall.at[lsrc(d), slot], fs.at[k, d], fr.at[k, d])

    for d in range(1, E):
        g_copy(d).start()
    for d in range(1, NL):
        f_copy(0, d).start()
    for k in range(1, E):
        g_in(k).wait_recv()
        for d in range(1, NL):
            f_copy(k, d).start()

    def rows_of(q):
        for i in range(E):
            xs[i * R:(i + 1) * R, :] = xall[q, i].astype(F32)
        return xs[...]

    def p_copy(c, d):
        return to_lat(d, psend.at[c, d], precv.at[c, d], ps.at[c, d], pr.at[c, d])

    x_own = rows_of(l).astype(BF16)
    for c in range(NC):
        w_enc[c].wait()
        part = jnp.dot(x_own, wenc_v[c], preferred_element_type=F32)
        for q in range(NL):
            psc[q] = part[q * Tl:(q + 1) * Tl, :]
        for d in range(1, NL):
            psend[c, d] = psc[lpeer(d)].astype(BF16)
            p_copy(c, d).start()
        own[c] = psc[l]

    for k in range(E):
        for d in range(1, NL):
            f_in(k, d).wait_recv()
    x_full = jnp.concatenate([rows_of(q) for q in range(NL)], axis=1).astype(BF16)
    w_g.wait()
    gate_sum = dot_nt(x_full, wg_v[...])
    w_u.wait()
    up_sum = dot_nt(x_full, wu_v[...])
    hidden = (gate_sum * jax.nn.sigmoid(1.702 * gate_sum) * (up_sum + 1.0)).astype(BF16)

    def c_copy(c, d):
        return to_lat(d, call.at[c, l], call.at[c, l], cs.at[c, d], cr.at[c, d])

    def c_in(c, d):
        return to_lat(d, call.at[c, lsrc(d)], call.at[c, lsrc(d)], cs.at[c, d], cr.at[c, d])

    def finish_codes(c):
        pre = own[c]
        for d in range(1, NL):
            p_copy(c, d).wait_recv()
            pre = pre + precv[c, d].astype(F32)
        code = jnp.maximum(pre + benc[:, c * CW:(c + 1) * CW], 0.0).astype(BF16)
        call[c, l] = code
        codes_ref[:, c * CW:(c + 1) * CW] = code
        for d in range(1, NL):
            c_copy(c, d).start()

    for c in range(NC // 2):
        finish_codes(c)

    def h_copy(d):
        return to_lat(d, msend.at[d], mrecv.at[d], hs.at[d], hr.at[d])

    w_d.wait()
    part = jnp.dot(hidden, wd_v[...], preferred_element_type=F32)
    for q in range(NL):
        phs[q] = part[:, q * Dl:(q + 1) * Dl]
    for d in range(1, NL):
        msend[d] = phs[lpeer(d)].astype(BF16)
        h_copy(d).start()
    for c in range(NC // 2, NC):
        finish_codes(c)

    def a_copy(d):
        return to_exp(d, ras.at[peer(d)], rar.at[d], as_.at[d], ar.at[d])

    def z_copy(d):
        return to_exp(d, rbs.at[peer(d)], rbr.at[d], zs.at[d], zr.at[d])

    def b_copy(d):
        return to_exp(d, mbs.at[peer(d)], mbr.at[d], bs.at[d], br.at[d])

    def codes_of(c):
        return call[c].reshape(T, CW)

    def add(c, low, high):
        term = dot_nt(codes_of(c), wdec_v[c, low:high, :])
        if c == 0:
            racc[:, low:high] = term
        else:
            racc[:, low:high] += term

    def arrive(c):
        for d in range(1, NL):
            c_in(c, d).wait_recv()
        w_dec[c].wait()

    for c in range(NC // 2):
        arrive(c)
        add(c, 0, N1)
        add(c, N1, Dl)

    total = phs[l]
    for d in range(1, NL):
        h_copy(d).wait_recv()
        total = total + mrecv[d].astype(F32)
    ms[...] = total
    for i in range(E):
        mbs[i] = ms[i * R:(i + 1) * R, :].astype(BF16)
    for d in range(1, E):
        b_copy(d).start()

    for c in range(NC // 2, NC):
        arrive(c)
        add(c, 0, N1)
        if c == NC - 1:
            for i in range(E):
                ras[i] = racc[i * R:(i + 1) * R, 0:N1].astype(BF16)
            for d in range(1, E):
                a_copy(d).start()
        add(c, N1, Dl)
    for i in range(E):
        rbs[i] = racc[i * R:(i + 1) * R, N1:Dl].astype(BF16)
    for d in range(1, E):
        z_copy(d).start()

    eye = lax.broadcasted_iota(jnp.int32, (R, R), 0) == lax.broadcasted_iota(jnp.int32, (R, R), 1)

    def weight_of(e):
        line = jnp.sum(jnp.where(routes[...] == e, gates[...], 0.0), axis=0, keepdims=True)
        return jnp.sum(jnp.where(eye, jnp.broadcast_to(line, (R, R)), 0.0), axis=1, keepdims=True)

    mine = pl.ds(pl.multiple_of(me * R, R), R)
    moe = weight_of(me) * ms[mine, :]
    for d in range(1, E):
        b_copy(d).wait_recv()
        moe = moe + weight_of(src(d)) * mbr[d].astype(F32)
    moe = moe.astype(BF16)
    moe_ref[...] = moe
    err_ref[...] = moe.astype(F32) - bdec[...].reshape(1, Dl)

    first = racc[mine, 0:N1]
    for d in range(1, E):
        a_copy(d).wait_recv()
        first = first + rar[d].astype(F32)
    err_ref[:, 0:N1] = err_ref[:, 0:N1] - first
    last = racc[mine, N1:Dl]
    for d in range(1, E):
        z_copy(d).wait_recv()
        last = last + rbr[d].astype(F32)
    err_ref[:, N1:Dl] = err_ref[:, N1:Dl] - last

    for d in range(1, E):
        g_copy(d).wait_send()
        a_copy(d).wait_send()
        b_copy(d).wait_send()
        z_copy(d).wait_send()
    for d in range(1, NL):
        for k in range(E):
            f_copy(k, d).wait_send()
        for c in range(NC):
            p_copy(c, d).wait_send()
            c_copy(c, d).wait_send()
        h_copy(d).wait_send()


def hand_over(a, b, c, a_out, b_out, c_out):
    a_out[...] = a[...]
    b_out[...] = b[...]
    c_out[...] = c[...]


def per_device(E, NL, tokens, routes, gates, w_gate, w_up, w_down, w_enc, b_enc, w_dec, b_dec):
    R, Dl = tokens.shape
    D = w_down.shape[2]
    F = w_down.shape[1]
    Lc = w_enc.shape[1]
    NC = CHUNKS
    CW = Lc // NC
    T = E * R
    Tl = T // NL
    N1 = pl.cdiv(pl.cdiv(Dl, 2), 128) * 128
    N2 = Dl - N1
    hbm = pl.BlockSpec(memory_space=pl.ANY)
    vmem = pl.BlockSpec(memory_space=pltpu.VMEM)
    dma = pltpu.SemaphoreType.DMA
    results = pl.pallas_call(
        functools.partial(kernel, E, NL),
        out_shape=(
            jax.ShapeDtypeStruct((R, Dl), BF16),
            jax.ShapeDtypeStruct((Tl, Lc), BF16),
            jax.ShapeDtypeStruct((R, Dl), F32),
        ),
        in_specs=[vmem, vmem, vmem, hbm, vmem, hbm, hbm, hbm, hbm, vmem],
        out_specs=(vmem, vmem, vmem),
        scratch_shapes=[
            pltpu.VMEM((NC, Dl, CW), BF16),
            pltpu.VMEM((F, D), BF16),
            pltpu.VMEM((F, D), BF16),
            pltpu.VMEM((F, D), BF16),
            pltpu.VMEM((NC, Dl, CW), BF16),
            pltpu.VMEM((NL, E, R, Dl), BF16),
            pltpu.VMEM((T, Dl), F32),
            pltpu.VMEM((NL, Tl, CW), F32),
            pltpu.VMEM((NC, Tl, CW), F32),
            pltpu.VMEM((NC, NL, Tl, CW), BF16),
            pltpu.VMEM((NC, NL, Tl, CW), BF16),
            pltpu.VMEM((NC, NL, Tl, CW), BF16),
            pltpu.VMEM((NL, T, Dl), F32),
            pltpu.VMEM((NL, T, Dl), BF16),
            pltpu.VMEM((NL, T, Dl), BF16),
            pltpu.VMEM((T, Dl), F32),
            pltpu.VMEM((E, R, Dl), BF16),
            pltpu.VMEM((E, R, Dl), BF16),
            pltpu.VMEM((T, Dl), F32),
            pltpu.VMEM((E, R, N1), BF16),
            pltpu.VMEM((E, R, N1), BF16),
            pltpu.VMEM((E, R, N2), BF16),
            pltpu.VMEM((E, R, N2), BF16),
            dma((2 * NC + 3,)),
            dma((E,)), dma((E,)),
            dma((E, NL)), dma((E, NL)),
            dma((NC, NL)), dma((NC, NL)),
            dma((NC, NL)), dma((NC, NL)),
            dma((NL,)), dma((NL,)),
            dma((E,)), dma((E,)),
            dma((E,)), dma((E,)),
            dma((E,)), dma((E,)),
        ],
        compiler_params=pltpu.CompilerParams(
            collective_id=0, has_side_effects=True, vmem_limit_bytes=58 * 1024 * 1024
        ),
    )(
        tokens, routes.T, gates.T, w_enc, b_enc.reshape(1, -1),
        w_gate[0].T, w_up[0].T, w_down[0], w_dec.T, b_dec,
    )
    return pl.pallas_call(
        hand_over,
        out_shape=tuple(jax.ShapeDtypeStruct(r.shape, r.dtype) for r in results),
        in_specs=[vmem] * 3,
        out_specs=(vmem,) * 3,
    )(*results)


def solution(mesh):
    placed = (
        P(("grp", "exp"), "lat"),
        P(("grp", "exp"), None),
        P(("grp", "exp"), None),
        P("exp", None, "lat"),
        P("exp", None, "lat"),
        P("exp", "lat", None),
        P("lat", "exp"),
        P("exp"),
        P("exp", "lat"),
        P("lat"),
    )
    return jax.shard_map(
        functools.partial(per_device, mesh.shape["exp"], mesh.shape["lat"]),
        mesh=mesh,
        in_specs=placed,
        out_specs=(P(("grp", "exp"), "lat"), P(("grp", "lat"), "exp"), P(("grp", "exp"), "lat")),
        check_vma=False,
    )
```
